256 devices in a mesh: seq: 128 (over x, z, y), head: 2 (over core).
Axes of the slice: x: 4, y: 4, z: 8, core: 2. Of those that a mesh axis runs over, the one named last changes fastest.
Arguments:
- q_raster: bfloat16 [65536, 2048], P('seq', 'head'), may hold values from -11 to 11
- k_raster: bfloat16 [65536, 2048], P('seq', 'head'), may hold values from -11 to 11
- v_raster: bfloat16 [65536, 2048], P('seq', 'head'), may hold values from -15 to 15
- hilbert_order: int32 [65536], P('seq'), may hold values from 0 to 65535, as said below
- key_blocks: int32 [128, 8], P('seq'), may hold values from 0 to 127, as said below
- out_weight: bfloat16 [2048, 2048], P('head'), may hold values from -0.125 to 0.125
Outputs:
- projected: bfloat16 [65536, 2048], P(('seq', 'head'))
The draws below stay inside these ranges and needn't reach their ends.
Inputs may be any that keep to these rules, and one draw needn't show every extreme that they name: `hilbert_order`: the image is 256 patches wide, and raster row r is line r // 256, column r % 256. Aligned range t of 1024 positions holds, in some order, exactly the rows of the square tile of lines (t // 8) * 32 onward and columns (t % 8) * 32 onward, 32 of each. `key_blocks`: row b lists b, b - 1 and b + 1 (modulo 128) in slots 0, 1 and 2, then other blocks; the 8 entries of a row are distinct.
All inputs are finite; a program needn't handle non-finite values.
Results may differ from the reference program's by a relative error of at most 0.0053.
Values may be sent and summed in bfloat16 or wider, within the bound.
No kernel may reach another device: no remote copies, remote signals or barrier semaphores. Data moves between devices by JAX's collectives and lax.ppermute only.
A program may use at most 128 MiB of HBM per device.

```python
import math
import jax
import jax.numpy as jnp
from jax import lax

TILE = 32
TCOLS = 8
HEADS = 16
HD = 128
SEL = 8
OUTW = 2048
BLOCK = 512
BLOCK_TOTAL = 128
TOKENS = 65536
F = 2048


def hilbert_cells(side):
    position = jnp.arange(side * side, dtype=jnp.int32)
    column_pos = jnp.zeros_like(position)
    row_pos = jnp.zeros_like(position)
    remaining = position
    for level in range(side.bit_length() - 1):
        span_size = 2 ** level
        bit_x = remaining // 2 % 2
        bit_y = (remaining ^ bit_x) % 2
        flip_both = (bit_y == 0) & (bit_x == 1)
        column_pos = jnp.where(flip_both, span_size - 1 - column_pos, column_pos)
        row_pos = jnp.where(flip_both, span_size - 1 - row_pos, row_pos)
        do_swap = bit_y == 0
        column_pos, row_pos = (jnp.where(do_swap, row_pos, column_pos), jnp.where(do_swap, column_pos, row_pos))
        column_pos = column_pos + span_size * bit_x
        row_pos = row_pos + span_size * bit_y
        remaining = remaining // 4
    return (column_pos, row_pos)


def draw_q_raster(key, part):
    key = jax.random.fold_in(key, 5)
    values = 1.5 * jax.random.truncated_normal(key, -6.0, 6.0, (TOKENS, F), jnp.float32)
    return values.astype(jnp.bfloat16)


def draw_k_raster(key, part):
    key = jax.random.fold_in(key, 7)
    values = 1.5 * jax.random.truncated_normal(key, -6.0, 6.0, (TOKENS, F), jnp.float32)
    return values.astype(jnp.bfloat16)


def draw_hilbert_order(key, part):
    key = jax.random.fold_in(key, 11)
    tile_count = TOKENS // (TILE * TILE)
    image_width = TILE * TCOLS
    column_pos, row_pos = hilbert_cells(TILE)
    orient = jax.random.randint(key, (tile_count, 1), 0, 8)
    transpose_bit = orient % 2
    flip_column = orient // 2 % 2
    flip_row = orient // 4 % 2
    column_now = jnp.where(transpose_bit == 1, row_pos[None, :], column_pos[None, :])
    row_now = jnp.where(transpose_bit == 1, column_pos[None, :], row_pos[None, :])
    column_now = jnp.where(flip_column == 1, TILE - 1 - column_now, column_now)
    row_now = jnp.where(flip_row == 1, TILE - 1 - row_now, row_now)
    tile_ids = jnp.arange(tile_count, dtype=jnp.int32)[:, None]
    tile_line = tile_ids // TCOLS
    tile_column = tile_ids % TCOLS
    raster = (tile_line * TILE + row_now) * image_width + tile_column * TILE + column_now
    return raster.reshape(TOKENS).astype(jnp.int32)


def draw_key_blocks(key, part):
    key = jax.random.fold_in(key, 23)
    key_favored, key_noise = jax.random.split(key)
    block_numbers = jnp.arange(BLOCK_TOTAL, dtype=jnp.int32)
    favored_boost = (jax.random.randint(key_favored, (BLOCK_TOTAL,), 0, 8) == 0).astype(jnp.int32) * BLOCK_TOTAL
    random_jitter = jax.random.randint(key_noise, (BLOCK_TOTAL, BLOCK_TOTAL), 0, BLOCK_TOTAL)
    block_ranking = (random_jitter + favored_boost[None, :]) * BLOCK_TOTAL + block_numbers[None, :]
    offset = (block_numbers[None, :] - block_numbers[:, None]) % BLOCK_TOTAL
    nearby = (offset == 0) | (offset == 1) | (offset == BLOCK_TOTAL - 1)
    block_ranking = jnp.where(nearby, -1, block_ranking)
    top_scores, picked = lax.top_k(block_ranking, SEL - 3)
    lists = jnp.concatenate([block_numbers[:, None], ((block_numbers - 1) % BLOCK_TOTAL)[:, None], ((block_numbers + 1) % BLOCK_TOTAL)[:, None], picked.astype(jnp.int32)], axis=1)
    return lists.astype(jnp.int32)


def shard_levels(stream_key, extent, shards, smallest, top_value):
    factor_of = 1.0
    for dim, blocks in shards:
        heights = jax.random.uniform(jax.random.fold_in(jax.random.fold_in(stream_key, 6), dim), (blocks,), jnp.float32, smallest / len(shards), top_value / len(shards))
        factor_of = factor_of * jnp.repeat(jnp.exp(heights), extent[dim] // blocks).reshape((-1,) + (1,) * (len(extent) - 1 - dim))
    return factor_of


def normal_values(rng, shape, deviation, most, shards=(), held_as=jnp.bfloat16):
    result = deviation * jax.random.normal(rng, shape, jnp.float32)
    if shards:
        result = result * shard_levels(rng, shape, shards, -0.22, 0.18)
    return jnp.clip(result, -most, most).astype(held_as)


def setup_inputs(seed: int = 0) -> dict:
    splits = jax.random.split(jax.random.key(seed), 7)
    q_raster = draw_q_raster(jax.random.fold_in(splits[6], 71), 0)
    k_raster = draw_k_raster(jax.random.fold_in(splits[6], 71), 0)
    v_raster = normal_values(splits[2], (TOKENS, F), 2.5, 15.0, ((0, 128), (1, 2)))
    hilbert_order = draw_hilbert_order(jax.random.fold_in(splits[6], 71), 0)
    key_blocks = draw_key_blocks(jax.random.fold_in(splits[6], 71), 0)
    out_weight = normal_values(splits[5], (F, OUTW), F ** -0.5, 0.125, ((0, 2),))
    return dict(q_raster=q_raster, k_raster=k_raster, v_raster=v_raster, hilbert_order=hilbert_order, key_blocks=key_blocks, out_weight=out_weight)


def reference(q_raster, k_raster, v_raster, hilbert_order, key_blocks, out_weight):
    query = q_raster[hilbert_order]
    keys_all = k_raster[hilbert_order]
    values_all = v_raster[hilbert_order]
    score_scale = 1.0 / math.sqrt(HD)
    query_blocks = query.reshape(BLOCK_TOTAL, BLOCK, F)
    key_tiles = keys_all.reshape(BLOCK_TOTAL, BLOCK, F)
    value_tiles = values_all.reshape(BLOCK_TOTAL, BLOCK, F)

    def one_block(pair_args):
        query_block, block_list = pair_args
        keys_here = key_tiles[block_list].reshape(SEL * BLOCK, HEADS, HD).astype(jnp.float32)
        values_here = value_tiles[block_list].reshape(SEL * BLOCK, HEADS, HD).astype(jnp.float32)
        query_here = query_block.reshape(BLOCK, HEADS, HD).astype(jnp.float32)
        scores = jnp.einsum('qhd,khd->hqk', query_here, keys_here) * score_scale
        row_max = lax.optimization_barrier(jnp.max(scores, axis=-1, keepdims=True))
        weights = jnp.exp(scores - row_max)
        totals = lax.optimization_barrier(jnp.sum(weights, axis=-1))
        probs = lax.optimization_barrier(weights.astype(jnp.bfloat16)).astype(jnp.float32)
        mixed = jnp.einsum('hqk,khd->qhd', probs, values_here)
        mixed = mixed / jnp.transpose(totals)[:, :, None]
        return mixed.reshape(BLOCK, F).astype(jnp.bfloat16)
    attended = lax.map(one_block, (query_blocks, key_blocks)).reshape(TOKENS, F)
    return jnp.dot(attended, out_weight, preferred_element_type=jnp.float32).astype(jnp.bfloat16)
```

```python
import functools
import math

import jax
import jax.numpy as jnp
from jax import lax
from jax.experimental import pallas as pl
from jax.experimental.pallas import tpu as pltpu
from jax.sharding import Mesh, PartitionSpec as P

TILE = 32
TCOLS = 8
HD = 128
SEL = 8
BLOCK = 512
PART = 128
SEQ = ("x", "zh", "zl", "yh", "yl")
LINE = ("zh", "zl")
PLANE = ("x", "yh", "yl")
BAND = ("zl", "yh", "yl")
SIZES = (4, 2, 4, 2, 2, 2)
CHUNKS = (1, 1, 1, 1)
VMEM_LIMIT = 48 * 1024 * 1024


def exchange(value, axes):
    return lax.all_to_all(value, axes, split_axis=0, concat_axis=0, tiled=True)


def picked(row, width):
    col = jnp.transpose(jnp.broadcast_to(row, (128, BLOCK)))
    lane = lax.broadcasted_iota(jnp.int32, (BLOCK, 128), 1)
    parts = [
        jnp.where(col == lane + 128 * k, 1.0, 0.0).astype(jnp.bfloat16) for k in range(width // 128)
    ]
    return jnp.concatenate(parts, axis=1)


def order_kv_kernel(place_ref, rows_ref, out_ref):
    tile = rows_ref[...].reshape(TILE * TILE, HD)
    for b in range(2):
        hot = picked(place_ref[0, b : b + 1, :], TILE * TILE)
        rows = jnp.dot(hot, tile, preferred_element_type=jnp.float32).astype(jnp.bfloat16)
        out_ref[:, b] = rows.reshape(4, PART, HD)


def order_kv(place, rows, tiles):
    return pl.pallas_call(
        order_kv_kernel,
        grid=(tiles,),
        in_specs=[
            pl.BlockSpec((1, 2, BLOCK), lambda t: (t, 0, 0)),
            pl.BlockSpec((TILE, 1, TILE, HD), lambda t: (0, t, 0, 0)),
        ],
        out_specs=pl.BlockSpec((4, 2, PART, HD), lambda t: (0, t, 0, 0)),
        out_shape=jax.ShapeDtypeStruct((4, 2 * tiles, PART, HD), jnp.bfloat16),
        compiler_params=pltpu.CompilerParams(vmem_limit_bytes=VMEM_LIMIT),
        cost_estimate=pl.CostEstimate(
            flops=tiles * 4 * BLOCK * TILE * TILE * HD, bytes_accessed=tiles * 2**19, transcendentals=0
        ),
        name="order_kv",
    )(place, rows)


def order_q_kernel(place_ref, near_ref, far_ref, out_ref):
    hot = picked(place_ref[...], 2 * BLOCK)
    rows = jnp.dot(hot[:, :BLOCK], near_ref[...], preferred_element_type=jnp.float32)
    rows += jnp.dot(hot[:, BLOCK:], far_ref[...], preferred_element_type=jnp.float32)
    out_ref[...] = rows.astype(jnp.bfloat16)


def order_q(place, near, far):
    width = near.shape[1]
    return pl.pallas_call(
        order_q_kernel,
        grid=(2,),
        in_specs=[
            pl.BlockSpec((1, BLOCK), lambda t: (0, 0)),
            pl.BlockSpec((BLOCK, width // 2), lambda t: (0, t)),
            pl.BlockSpec((BLOCK, width // 2), lambda t: (0, t)),
        ],
        out_specs=pl.BlockSpec((BLOCK, width // 2), lambda t: (0, t)),
        out_shape=jax.ShapeDtypeStruct((BLOCK, width), jnp.bfloat16),
        compiler_params=pltpu.CompilerParams(vmem_limit_bytes=VMEM_LIMIT),
        cost_estimate=pl.CostEstimate(
            flops=4 * BLOCK * BLOCK * width, bytes_accessed=3 * 2**20, transcendentals=0
        ),
        name="order_q",
    )(place, near, far)


def select_kernel(blocks_ref, held_ref, out_ref, sem, *, per_group):
    def send(step, carry):
        reader = step // SEL
        slot = step % SEL
        block = blocks_ref[reader, slot]
        col = lax.shift_right_logical(block, 5)
        half = lax.shift_right_logical(block, 4) & 1
        group = (block & 15) // per_group
        place = (block & 15) % per_group
        pltpu.make_async_copy(
            held_ref.at[half, :, group, col, place], out_ref.at[reader, :, slot], sem
        ).start()
        return carry

    lax.fori_loop(0, 16 * SEL, send, 0)
    pltpu.make_async_copy(out_ref, out_ref, sem).wait()


def select(blocks, held):
    half, slabs, groups, cols, per_group = held.shape[:5]
    return pl.pallas_call(
        functools.partial(select_kernel, per_group=per_group),
        grid_spec=pltpu.PrefetchScalarGridSpec(
            num_scalar_prefetch=1,
            grid=(1,),
            in_specs=[pl.BlockSpec(memory_space=pl.ANY)],
            out_specs=pl.BlockSpec((16, slabs, SEL, PART, HD), lambda g, blocks: (0, 0, 0, 0, 0)),
            scratch_shapes=[pltpu.SemaphoreType.DMA],
        ),
        out_shape=jax.ShapeDtypeStruct((16, slabs, SEL, PART, HD), jnp.bfloat16),
        compiler_params=pltpu.CompilerParams(vmem_limit_bytes=VMEM_LIMIT),
        cost_estimate=pl.CostEstimate(
            flops=0, bytes_accessed=slabs * 2**23, transcendentals=0
        ),
        name="select",
    )(blocks, held)


def attend_kernel(q_ref, k_ref, v_ref, out_ref, *, scale):
    sub = BLOCK // 2
    for r in range(2):
        query = q_ref[r * sub : (r + 1) * sub, :]
        top = jnp.full((sub, 1), -jnp.inf, jnp.float32)
        total = jnp.zeros((sub, 1), jnp.float32)
        mixed = jnp.zeros((sub, HD), jnp.float32)
        for c in range(4):
            keys = k_ref[c, 0, 0, 0]
            values = v_ref[c, 0, 0, 0]
            scores = lax.dot_general(
                query, keys, (((1,), (1,)), ((), ())), preferred_element_type=jnp.float32
            )
            peak = jnp.maximum(top, jnp.max(scores, axis=1, keepdims=True))
            weights = jnp.exp2(scores * scale - peak * scale)
            fade = jnp.exp2((top - peak) * scale)
            total = total * fade + jnp.sum(weights, axis=1, keepdims=True)
            mixed = mixed * fade + jnp.dot(
                weights.astype(jnp.bfloat16), values, preferred_element_type=jnp.float32
            )
            top = peak
        out_ref[r * sub : (r + 1) * sub, :] = (mixed / total).astype(jnp.bfloat16)


def attend(query, fetched, first, slabs):
    rows = SEL * PART
    spec = (4, 1, 1, 1, rows, HD)
    heads = 2 * slabs
    return pl.pallas_call(
        functools.partial(attend_kernel, scale=math.log2(math.e) / math.sqrt(HD)),
        grid=(heads,),
        in_specs=[
            pl.BlockSpec((BLOCK, HD), lambda g: (0, first + g)),
            pl.BlockSpec(spec, lambda g: (0, g % 2, 0, g // 2, 0, 0)),
            pl.BlockSpec(spec, lambda g: (0, g % 2, 1, g // 2, 0, 0)),
        ],
        out_specs=pl.BlockSpec((BLOCK, HD), lambda g: (0, g)),
        out_shape=jax.ShapeDtypeStruct((BLOCK, heads * HD), jnp.bfloat16),
        compiler_params=pltpu.CompilerParams(vmem_limit_bytes=VMEM_LIMIT),
        cost_estimate=pl.CostEstimate(
            flops=heads * 4 * BLOCK * 4 * rows * HD * 4,
            bytes_accessed=heads * 2**21,
            transcendentals=heads * BLOCK * 4 * rows,
        ),
        name="attend",
    )(query, fetched, fetched)


def body(q_raster, k_raster, v_raster, hilbert_order, key_blocks, out_weight):
    width = q_raster.shape[1]
    image_width = TILE * TCOLS
    core = lax.axis_index("core")
    swap = [(0, 1), (1, 0)]
    weight_far = lax.ppermute(out_weight, "core", swap)

    in_tile = hilbert_order // image_width % TILE * TILE + hilbert_order % image_width % TILE
    band_places = exchange(jnp.broadcast_to(in_tile[None, None], (16, 1, BLOCK)), BAND)
    lists = exchange(jnp.broadcast_to(key_blocks[None], (16, 1, SEL)), PLANE).reshape(16, SEL)

    key_lines = k_raster.reshape(2, TCOLS, TILE, width // HD, HD)
    value_lines = v_raster.reshape(2, TCOLS, TILE, width // HD, HD)
    both = jnp.stack([key_lines, value_lines])
    line_pos = lax.axis_index("zl")

    fetched = []
    first = 0
    for slabs in CHUNKS:
        groups = 4 // slabs
        tiles = TCOLS // groups
        part = lax.slice_in_dim(both, first, first + 2 * slabs, axis=4)
        part = part.reshape(2, 2, groups, tiles, TILE, slabs, 2, HD)
        part = jnp.transpose(part, (5, 2, 6, 0, 1, 3, 4, 7)).reshape(16, 2, tiles, TILE, HD)
        rows = exchange(part, BAND).reshape(TILE, tiles, TILE, HD)
        group = line_pos % groups
        place = lax.dynamic_slice_in_dim(
            band_places.reshape(TCOLS, 2, BLOCK), group * tiles, tiles, axis=0
        )
        ordered = order_kv(place, rows, tiles)
        spread = exchange(ordered, "x")
        held = lax.all_gather(spread, LINE, axis=0)
        held = held.reshape(2, slabs, groups, 4, 2 * tiles, PART, HD)
        sent = select(lists, held)
        got = exchange(sent, PLANE)
        fetched.append((first, slabs, got.reshape(4, 2, 2, slabs, SEL * PART, HD)))
        first += 2 * slabs

    lines = q_raster.reshape(2, TCOLS, TILE, width)
    toward = jnp.transpose(lines, (1, 0, 2, 3))
    near = exchange(toward, ("zl", "yh")).reshape(BLOCK, width)
    far = lax.ppermute(near, "yl", swap)
    line = in_tile // TILE
    from_yl = line // 2 % 2
    q_place = (
        jnp.where(from_yl == lax.axis_index("yl"), 0, BLOCK)
        + (line // 8 * 2 + line // 4 % 2) * 64
        + line % 2 * TILE
        + in_tile % TILE
    )
    query = order_q(q_place[None], near, far)

    half = BLOCK // 2
    result = jnp.zeros((half, out_weight.shape[1]), jnp.float32)
    for first, slabs, got in fetched:
        attended = attend(query, got, first, slabs)
        mine = lax.dynamic_slice_in_dim(attended, core * half, half, axis=0)
        theirs = lax.dynamic_slice_in_dim(attended, (1 - core) * half, half, axis=0)
        other = lax.ppermute(theirs, "core", swap)
        feats = slice(first * HD, (first + 2 * slabs) * HD)
        result += jnp.dot(mine, out_weight[feats], preferred_element_type=jnp.float32)
        result += jnp.dot(other, weight_far[feats], preferred_element_type=jnp.float32)
    return result.astype(jnp.bfloat16)


def solution(mesh):
    split = Mesh(mesh.devices.reshape(SIZES), SEQ + ("core",))
    placed = (
        P(SEQ, "core"),
        P(SEQ, "core"),
        P(SEQ, "core"),
        P(SEQ),
        P(SEQ, None),
        P("core", None),
    )
    return jax.shard_map(
        body, mesh=split, in_specs=placed, out_specs=P(SEQ + ("core",), None), check_vma=False
    )
```

```python
import functools
import itertools
import math

import jax
import jax.numpy as jnp
from jax import lax
from jax.experimental import pallas as pl
from jax.experimental.pallas import tpu as pltpu
from jax.sharding import Mesh, PartitionSpec as P

TILE = 32
TCOLS = 8
HD = 128
SEL = 8
BLOCK = 512
PART = 128
SEQ = ("x", "zh", "zl", "yh", "yl")
LINE = ("zh", "zl")
PLANE = ("x", "yh", "yl")
BAND = ("zl", "yh", "yl")
SIZES = (4, 2, 4, 2, 2, 2)
CHUNKS = 4
LEAD = 1
TILES = 2
VMEM_LIMIT = 48 * 1024 * 1024


def exchange(value, axes):
    return lax.all_to_all(value, axes, split_axis=0, concat_axis=0, tiled=True)


def after(value, *earlier):
    return lax.optimization_barrier((value,) + earlier)[0]


def picked(row, width):
    col = jnp.transpose(jnp.broadcast_to(row, (128, BLOCK)))
    lane = lax.broadcasted_iota(jnp.int32, (BLOCK, 128), 1)
    parts = [
        jnp.where(col == lane + 128 * k, 1.0, 0.0).astype(jnp.bfloat16) for k in range(width // 128)
    ]
    return jnp.concatenate(parts, axis=1)


def pack_kernel(k_ref, v_ref, *refs, chunks):
    out_ref = refs[-1]
    line_rows = TILE * TCOLS
    pair = TILES * TILE
    for dest in range(16):
        group, head, kv = dest // 4, dest // 2 % 2, dest % 2
        from_ref = v_ref if kv else k_ref
        at = 0
        for c, line in itertools.product(range(chunks[0], chunks[1]), range(2)):
            cols = pl.ds((2 * (c - chunks[0]) + head) * HD, HD)
            rows = pl.ds(line * line_rows + group * pair, pair)
            out_ref[dest, pl.ds(at, pair), :] = from_ref[rows, cols]
            at += pair
        if len(refs) == 3:
            q_ref, places_ref = refs[:2]
            for h, line in itertools.product(range(4), range(2)):
                rows = pl.ds(line * line_rows + (dest // 2) * TILE, TILE)
                out_ref[dest, pl.ds(at, TILE), :] = q_ref[rows, pl.ds((4 * kv + h) * HD, HD)]
                at += TILE
            out_ref[dest, pl.ds(at, 16), :] = places_ref[...]


def pack(keys, values, chunks, *more):
    width = 2 * HD * (chunks[1] - chunks[0])
    part = pl.BlockSpec((BLOCK, width), lambda g: (0, 0))
    rows = 2 * TILES * TILE * (chunks[1] - chunks[0])
    more_specs = [pl.BlockSpec(m.shape, lambda g: (0, 0)) for m in more]
    if more:
        rows += 8 * TILE + 16
    if chunks[0]:
        keys, values = keys[:, chunks[0] * 2 * HD :], values[:, chunks[0] * 2 * HD :]
    return pl.pallas_call(
        functools.partial(pack_kernel, chunks=chunks),
        grid=(1,),
        in_specs=[part, part] + more_specs,
        out_specs=pl.BlockSpec((16, rows, HD), lambda g: (0, 0, 0)),
        out_shape=jax.ShapeDtypeStruct((16, rows, HD), jnp.bfloat16),
        compiler_params=pltpu.CompilerParams(vmem_limit_bytes=VMEM_LIMIT),
        cost_estimate=pl.CostEstimate(
            flops=0, bytes_accessed=2 * 16 * rows * HD * 2, transcendentals=0
        ),
        name="pack",
    )(keys, values, *more)


def order_kv_kernel(place_ref, rows_ref, out_ref):
    tile = rows_ref[...].reshape(TILE * TILE, HD)
    for b in range(2):
        hot = picked(place_ref[0, b : b + 1, :], TILE * TILE)
        rows = jnp.dot(hot, tile, preferred_element_type=jnp.float32).astype(jnp.bfloat16)
        out_ref[:, 0, b] = rows.reshape(4, PART, HD)


def order_kv(place, rows):
    chunks = rows.shape[1]
    return pl.pallas_call(
        order_kv_kernel,
        grid=(chunks, TILES),
        in_specs=[
            pl.BlockSpec((1, 2, BLOCK), lambda c, t: (t, 0, 0)),
            pl.BlockSpec((16, 1, 2, 1, TILE, HD), lambda c, t: (0, c, 0, t, 0, 0)),
        ],
        out_specs=pl.BlockSpec((4, 1, 2, PART, HD), lambda c, t: (0, c, t, 0, 0)),
        out_shape=jax.ShapeDtypeStruct((4, chunks, 2 * TILES, PART, HD), jnp.bfloat16),
        compiler_params=pltpu.CompilerParams(vmem_limit_bytes=VMEM_LIMIT),
        cost_estimate=pl.CostEstimate(
            flops=chunks * TILES * 4 * BLOCK * TILE * TILE * HD,
            bytes_accessed=chunks * TILES * 2**19,
            transcendentals=0,
        ),
        name="order_kv",
    )(place, rows)


def order_q_kernel(place_ref, rows_ref, out_ref):
    tile = rows_ref[...].reshape(TILE * TILE, HD)
    for b in range(2):
        hot = picked(place_ref[b : b + 1, :], TILE * TILE)
        out_ref[b, 0] = jnp.dot(hot, tile, preferred_element_type=jnp.float32).astype(jnp.bfloat16)


def order_q(place, rows):
    heads = rows.shape[1]
    return pl.pallas_call(
        order_q_kernel,
        grid=(heads,),
        in_specs=[
            pl.BlockSpec((2, BLOCK), lambda t: (0, 0)),
            pl.BlockSpec((16, 1, 2 * TILE, HD), lambda t: (0, t, 0, 0)),
        ],
        out_specs=pl.BlockSpec((2, 1, BLOCK, HD), lambda t: (0, t, 0, 0)),
        out_shape=jax.ShapeDtypeStruct((2, heads, BLOCK, HD), jnp.bfloat16),
        compiler_params=pltpu.CompilerParams(vmem_limit_bytes=VMEM_LIMIT),
        cost_estimate=pl.CostEstimate(
            flops=heads * 4 * BLOCK * TILE * TILE * HD, bytes_accessed=2**21, transcendentals=0
        ),
        name="order_q",
    )(place, rows)


def select_kernel(blocks_ref, held_ref, out_ref, sem):
    def send(step, carry):
        reader = step // SEL
        slot = step % SEL
        block = blocks_ref[reader, slot]
        col = lax.shift_right_logical(block, 5)
        line = lax.shift_right_logical(block, 2) & 7
        pltpu.make_async_copy(
            held_ref.at[line, col, block & 3], out_ref.at[reader, slot], sem
        ).start()
        return carry

    lax.fori_loop(0, 16 * SEL, send, 0)
    pltpu.make_async_copy(out_ref, out_ref, sem).wait()


def select(blocks, held):
    return pl.pallas_call(
        select_kernel,
        grid_spec=pltpu.PrefetchScalarGridSpec(
            num_scalar_prefetch=1,
            grid=(1,),
            in_specs=[pl.BlockSpec(memory_space=pl.ANY)],
            out_specs=pl.BlockSpec((16, SEL, PART, HD), lambda g, blocks: (0, 0, 0, 0)),
            scratch_shapes=[pltpu.SemaphoreType.DMA],
        ),
        out_shape=jax.ShapeDtypeStruct((16, SEL, PART, HD), jnp.bfloat16),
        compiler_params=pltpu.CompilerParams(vmem_limit_bytes=VMEM_LIMIT),
        cost_estimate=pl.CostEstimate(flops=0, bytes_accessed=2**23, transcendentals=0),
        name="select",
    )(blocks, held)


def attend_kernel(side_ref, q_ref, k_ref, v_ref, out_ref, *, scale):
    sub = BLOCK // 2
    for r in range(2):
        query = q_ref[0, 0, r * sub : (r + 1) * sub, :]
        top = jnp.full((sub, 1), -jnp.inf, jnp.float32)
        total = jnp.zeros((sub, 1), jnp.float32)
        mixed = jnp.zeros((sub, HD), jnp.float32)
        for c in range(4):
            keys = k_ref[c, 0, 0]
            values = v_ref[c, 0, 0]
            scores = lax.dot_general(
                query, keys, (((1,), (1,)), ((), ())), preferred_element_type=jnp.float32
            )
            peak = jnp.maximum(top, jnp.max(scores, axis=1, keepdims=True))
            weights = jnp.exp2(scores * scale - peak * scale)
            fade = jnp.exp2((top - peak) * scale)
            total = total * fade + jnp.sum(weights, axis=1, keepdims=True)
            mixed = mixed * fade + jnp.dot(
                weights.astype(jnp.bfloat16), values, preferred_element_type=jnp.float32
            )
            top = peak
        out_ref[r * sub : (r + 1) * sub, :] = (mixed / total).astype(jnp.bfloat16)


def attend(side, query, fetched, first):
    rows = SEL * PART
    spec = (4, 1, 1, rows, HD)
    heads = 2
    per_side = query.shape[1]
    return pl.pallas_call(
        functools.partial(attend_kernel, scale=math.log2(math.e) / math.sqrt(HD)),
        grid_spec=pltpu.PrefetchScalarGridSpec(
            num_scalar_prefetch=1,
            grid=(heads,),
            in_specs=[
                pl.BlockSpec(
                    (1, 1, BLOCK, HD),
                    lambda g, side: (first // per_side ^ side[0], first % per_side + g, 0, 0),
                ),
                pl.BlockSpec(spec, lambda g, side: (0, g, 0, 0, 0)),
                pl.BlockSpec(spec, lambda g, side: (0, g, 1, 0, 0)),
            ],
            out_specs=pl.BlockSpec((BLOCK, HD), lambda g, side: (0, g)),
        ),
        out_shape=jax.ShapeDtypeStruct((BLOCK, heads * HD), jnp.bfloat16),
        compiler_params=pltpu.CompilerParams(vmem_limit_bytes=VMEM_LIMIT),
        cost_estimate=pl.CostEstimate(
            flops=heads * 4 * BLOCK * 4 * rows * HD * 4,
            bytes_accessed=heads * 2**21,
            transcendentals=heads * BLOCK * 4 * rows,
        ),
        name="attend",
    )(side, query, fetched, fetched)


def body(q_raster, k_raster, v_raster, hilbert_order, key_blocks, out_weight):
    width = q_raster.shape[1]
    image_width = TILE * TCOLS
    core = lax.axis_index("core")
    swap = [(0, 1), (1, 0)]
    weight_far = lax.ppermute(out_weight, "core", swap)

    in_tile = hilbert_order // image_width % TILE * TILE + hilbert_order % image_width % TILE
    places = jnp.stack([in_tile // TILE, in_tile % TILE]).reshape(8, HD)
    listed = jnp.pad(key_blocks, ((0, 7), (0, HD - SEL)))
    places = jnp.concatenate([places, listed]).astype(jnp.bfloat16)
    by_chunk = (16, -1, 2, TILES, TILE, HD)
    kv_rows = 2 * TILES * TILE * LEAD
    lead = exchange(pack(k_raster, v_raster, (0, LEAD), q_raster, places), BAND)
    numbers = lead[:, -16:].astype(jnp.int32)
    band_places = numbers[:, :8].reshape(16, 2, BLOCK)
    band_places = (band_places[:, 0] * TILE + band_places[:, 1]).reshape(TCOLS, 2, BLOCK)
    line_pos = lax.axis_index("zl")
    place = lax.dynamic_slice_in_dim(band_places, line_pos * TILES, TILES, axis=0)
    ordered = order_kv(place, lead[:, :kv_rows].reshape(by_chunk))
    spread = exchange(ordered, "x")
    spreads = [spread[:, c] for c in range(LEAD)]

    lists = lax.dynamic_slice_in_dim(numbers[:, 8, :SEL], line_pos * 4, 4, axis=0)
    lists = [
        lax.ppermute(lists, "x", [(i, i ^ d) for i in range(4)]) if d else lists for d in range(4)
    ]
    lists = jnp.stack(lists)[lax.axis_index("x") ^ jnp.arange(4)].reshape(16, SEL)

    side = lax.axis_index("yl")
    tile_places = lax.dynamic_index_in_dim(band_places, lax.axis_index(("zl", "yh")), 0, False)
    tile_places = jnp.where(side == 0, tile_places, tile_places[::-1])
    q_ordered = order_q(tile_places, lead[:, kv_rows:-16].reshape(16, -1, 2 * TILE, HD))
    q_other = lax.ppermute(q_ordered[1], "yl", swap)
    query = jnp.stack([q_ordered[0], q_other])
    side = side.reshape(1)

    rest = exchange(after(pack(k_raster, v_raster, (LEAD, CHUNKS)), spread), BAND)
    ordered = order_kv(place, rest.reshape(by_chunk))
    later = exchange(after(ordered, lists, query), "x")
    spreads += [later[:, c] for c in range(CHUNKS - LEAD)]
    held = [lax.all_gather(part, LINE, axis=0) for part in spreads]

    half = BLOCK // 2
    results = [jnp.zeros((half, out_weight.shape[1]), jnp.float32)]
    for c in range(CHUNKS):
        ready = after(lists, *((results[c - 1],) if c > 1 else (later,)))
        got = exchange(select(ready, held[c]), PLANE)
        attended = attend(side, query, got.reshape(4, 2, 2, SEL * PART, HD), 2 * c)
        mine = lax.dynamic_slice_in_dim(attended, core * half, half, axis=0)
        theirs = lax.dynamic_slice_in_dim(attended, (1 - core) * half, half, axis=0)
        other = lax.ppermute(theirs, "core", swap)
        feats = slice(2 * c * HD, 2 * (c + 1) * HD)
        result = results[c] + jnp.dot(mine, out_weight[feats], preferred_element_type=jnp.float32)
        result += jnp.dot(other, weight_far[feats], preferred_element_type=jnp.float32)
        results.append(result)
    return results[-1].astype(jnp.bfloat16)


def solution(mesh):
    split = Mesh(mesh.devices.reshape(SIZES), SEQ + ("core",))
    placed = (
        P(SEQ, "core"),
        P(SEQ, "core"),
        P(SEQ, "core"),
        P(SEQ),
        P(SEQ, None),
        P("core", None),
    )
    return jax.shard_map(
        body, mesh=split, in_specs=placed, out_specs=P(SEQ + ("core",), None), check_vma=False
    )
```

```python
import functools
import itertools
import math

import jax
import jax.numpy as jnp
from jax import lax
from jax.experimental import pallas as pl
from jax.experimental.pallas import tpu as pltpu
from jax.sharding import Mesh, PartitionSpec as P

TILE = 32
TCOLS = 8
HD = 128
SEL = 8
BLOCK = 512
PART = 128
SEQ = ("x", "zh", "zl", "yh", "yl")
LINE = ("zh", "zl")
PLANE = ("x", "yh", "yl")
BAND = ("zl", "yh", "yl")
SIZES = (4, 2, 4, 2, 2, 2)
CHUNKS = 4
LEAD = 1
TILES = 2
VMEM_LIMIT = 48 * 1024 * 1024


def exchange(value, axes):
    return lax.all_to_all(value, axes, split_axis=0, concat_axis=0, tiled=True)


def after(value, *earlier):
    return lax.optimization_barrier((value,) + earlier)[0]


def swapped(pieces, axes):
    moved = [
        lax.ppermute(pieces[d], axes, [(i, i ^ d) for i in range(4)]) if d else pieces[0]
        for d in range(4)
    ]
    return jnp.stack(moved)


def picked(row, width):
    col = jnp.transpose(jnp.broadcast_to(row, (128, BLOCK)))
    lane = lax.broadcasted_iota(jnp.int32, (BLOCK, 128), 1)
    parts = [
        jnp.where(col == lane + 128 * k, 1.0, 0.0).astype(jnp.bfloat16) for k in range(width // 128)
    ]
    return jnp.concatenate(parts, axis=1)


def pack_kernel(k_ref, v_ref, *refs, chunks):
    out_ref = refs[-1]
    line_rows = TILE * TCOLS
    pair = TILES * TILE
    for dest in range(16):
        group, head, kv = dest // 4, dest // 2 % 2, dest % 2
        from_ref = v_ref if kv else k_ref
        at = 0
        for c, line in itertools.product(range(chunks[0], chunks[1]), range(2)):
            cols = pl.ds((2 * (c - chunks[0]) + head) * HD, HD)
            rows = pl.ds(line * line_rows + group * pair, pair)
            out_ref[dest, pl.ds(at, pair), :] = from_ref[rows, cols]
            at += pair
        if len(refs) == 3:
            q_ref, places_ref = refs[:2]
            for h, line in itertools.product(range(4), range(2)):
                rows = pl.ds(line * line_rows + (dest // 2) * TILE, TILE)
                out_ref[dest, pl.ds(at, TILE), :] = q_ref[rows, pl.ds((4 * kv + h) * HD, HD)]
                at += TILE
            out_ref[dest, pl.ds(at, 16), :] = places_ref[...]


def pack(keys, values, chunks, *more):
    width = 2 * HD * (chunks[1] - chunks[0])
    part = pl.BlockSpec((BLOCK, width), lambda g: (0, 0))
    rows = 2 * TILES * TILE * (chunks[1] - chunks[0])
    more_specs = [pl.BlockSpec(m.shape, lambda g: (0, 0)) for m in more]
    if more:
        rows += 8 * TILE + 16
    if chunks[0]:
        keys, values = keys[:, chunks[0] * 2 * HD :], values[:, chunks[0] * 2 * HD :]
    return pl.pallas_call(
        functools.partial(pack_kernel, chunks=chunks),
        grid=(1,),
        in_specs=[part, part] + more_specs,
        out_specs=pl.BlockSpec((16, rows, HD), lambda g: (0, 0, 0)),
        out_shape=jax.ShapeDtypeStruct((16, rows, HD), jnp.bfloat16),
        compiler_params=pltpu.CompilerParams(vmem_limit_bytes=VMEM_LIMIT),
        cost_estimate=pl.CostEstimate(
            flops=0, bytes_accessed=2 * 16 * rows * HD * 2, transcendentals=0
        ),
        name="pack",
    )(keys, values, *more)


def order_kv_kernel(place_ref, rows_ref, out_ref):
    tile = rows_ref[...].reshape(TILE * TILE, HD)
    for b in range(2):
        hot = picked(place_ref[0, b : b + 1, :], TILE * TILE)
        rows = jnp.dot(hot, tile, preferred_element_type=jnp.float32).astype(jnp.bfloat16)
        out_ref[:, 0, b] = rows.reshape(4, PART, HD)


def order_kv(place, rows):
    chunks = rows.shape[1]
    return pl.pallas_call(
        order_kv_kernel,
        grid=(chunks, TILES),
        in_specs=[
            pl.BlockSpec((1, 2, BLOCK), lambda c, t: (t, 0, 0)),
            pl.BlockSpec((16, 1, 2, 1, TILE, HD), lambda c, t: (0, c, 0, t, 0, 0)),
        ],
        out_specs=pl.BlockSpec((4, 1, 2, PART, HD), lambda c, t: (0, c, t, 0, 0)),
        out_shape=jax.ShapeDtypeStruct((4, chunks, 2 * TILES, PART, HD), jnp.bfloat16),
        compiler_params=pltpu.CompilerParams(vmem_limit_bytes=VMEM_LIMIT),
        cost_estimate=pl.CostEstimate(
            flops=chunks * TILES * 4 * BLOCK * TILE * TILE * HD,
            bytes_accessed=chunks * TILES * 2**19,
            transcendentals=0,
        ),
        name="order_kv",
    )(place, rows)


def order_q_kernel(place_ref, rows_ref, out_ref):
    tile = rows_ref[...].reshape(TILE * TILE, HD)
    for b in range(2):
        hot = picked(place_ref[b : b + 1, :], TILE * TILE)
        out_ref[b, 0] = jnp.dot(hot, tile, preferred_element_type=jnp.float32).astype(jnp.bfloat16)


def order_q(place, rows):
    heads = rows.shape[1]
    return pl.pallas_call(
        order_q_kernel,
        grid=(heads,),
        in_specs=[
            pl.BlockSpec((2, BLOCK), lambda t: (0, 0)),
            pl.BlockSpec((16, 1, 2 * TILE, HD), lambda t: (0, t, 0, 0)),
        ],
        out_specs=pl.BlockSpec((2, 1, BLOCK, HD), lambda t: (0, t, 0, 0)),
        out_shape=jax.ShapeDtypeStruct((2, heads, BLOCK, HD), jnp.bfloat16),
        compiler_params=pltpu.CompilerParams(vmem_limit_bytes=VMEM_LIMIT),
        cost_estimate=pl.CostEstimate(
            flops=heads * 4 * BLOCK * TILE * TILE * HD, bytes_accessed=2**21, transcendentals=0
        ),
        name="order_q",
    )(place, rows)


def select_kernel(blocks_ref, flip_ref, held_ref, out_ref, sem):
    def send(reader, carry):
        for slot in range(1, SEL):
            block = blocks_ref[reader, slot]
            col = lax.shift_right_logical(block, 5) ^ flip_ref[0]
            line = lax.shift_right_logical(block, 2) & 7
            pltpu.make_async_copy(
                held_ref.at[line, col, block & 3], out_ref.at[reader, slot - 1], sem
            ).start()
        return carry

    lax.fori_loop(0, 16, send, 0)
    pltpu.make_async_copy(out_ref, out_ref, sem).wait()


def select(blocks, flip, held):
    shape = (16, SEL - 1, PART, HD)
    return pl.pallas_call(
        select_kernel,
        grid_spec=pltpu.PrefetchScalarGridSpec(
            num_scalar_prefetch=2,
            grid=(1,),
            in_specs=[pl.BlockSpec(memory_space=pl.ANY)],
            out_specs=pl.BlockSpec(shape, lambda g, blocks, flip: (0, 0, 0, 0)),
            scratch_shapes=[pltpu.SemaphoreType.DMA],
        ),
        out_shape=jax.ShapeDtypeStruct(shape, jnp.bfloat16),
        compiler_params=pltpu.CompilerParams(vmem_limit_bytes=VMEM_LIMIT),
        cost_estimate=pl.CostEstimate(flops=0, bytes_accessed=2**23, transcendentals=0),
        name="select",
    )(blocks, flip, held)


def attend_kernel(pos_ref, q_ref, k_ref, v_ref, own_k_ref, own_v_ref, out_ref, *, scale):
    query = q_ref[0, 0]
    top = jnp.full((BLOCK, 1), -jnp.inf, jnp.float32)
    total = jnp.zeros((BLOCK, 1), jnp.float32)
    mixed = jnp.zeros((BLOCK, HD), jnp.float32)
    for c in range(4):
        keys = jnp.concatenate([k_ref[c, 0, 0], own_k_ref[0, c, 0]])
        values = jnp.concatenate([v_ref[c, 0, 0], own_v_ref[0, c, 0]])
        scores = lax.dot_general(
            query, keys, (((1,), (1,)), ((), ())), preferred_element_type=jnp.float32
        )
        peak = jnp.maximum(top, jnp.max(scores, axis=1, keepdims=True))
        weights = jnp.exp2(scores * scale - peak * scale)
        fade = jnp.exp2((top - peak) * scale)
        total = total * fade + jnp.sum(weights, axis=1, keepdims=True)
        mixed = mixed * fade + jnp.dot(
            weights.astype(jnp.bfloat16), values, preferred_element_type=jnp.float32
        )
        top = peak
    out_ref[...] = (mixed / total).astype(jnp.bfloat16)


def attend(pos, query, fetched, own, chunk):
    rows = (SEL - 1) * PART
    spec = (4, 1, 1, rows, HD)
    own_spec = (1, 4, 1, PART, HD)
    heads = 2
    per_side = query.shape[1]
    first = heads * chunk
    return pl.pallas_call(
        functools.partial(attend_kernel, scale=math.log2(math.e) / math.sqrt(HD)),
        grid_spec=pltpu.PrefetchScalarGridSpec(
            num_scalar_prefetch=1,
            grid=(heads,),
            in_specs=[
                pl.BlockSpec(
                    (1, 1, BLOCK, HD),
                    lambda g, pos: (first // per_side ^ (pos[0] & 1), first % per_side + g, 0, 0),
                ),
                pl.BlockSpec(spec, lambda g, pos: (0, g, 0, 0, 0)),
                pl.BlockSpec(spec, lambda g, pos: (0, g, 1, 0, 0)),
                pl.BlockSpec(own_spec, lambda g, pos: ((2 * g) ^ pos[0], 0, chunk, 0, 0)),
                pl.BlockSpec(own_spec, lambda g, pos: ((2 * g + 1) ^ pos[0], 0, chunk, 0, 0)),
            ],
            out_specs=pl.BlockSpec((BLOCK, HD), lambda g, pos: (0, g)),
        ),
        out_shape=jax.ShapeDtypeStruct((BLOCK, heads * HD), jnp.bfloat16),
        compiler_params=pltpu.CompilerParams(vmem_limit_bytes=VMEM_LIMIT),
        cost_estimate=pl.CostEstimate(
            flops=heads * 4 * BLOCK * BLOCK * SEL * HD * 4,
            bytes_accessed=heads * 2**21,
            transcendentals=heads * BLOCK * BLOCK * SEL,
        ),
        name="attend",
    )(pos, query, fetched, fetched, own, own)


def body(q_raster, k_raster, v_raster, hilbert_order, key_blocks, out_weight):
    width = q_raster.shape[1]
    image_width = TILE * TCOLS
    core = lax.axis_index("core")
    swap = [(0, 1), (1, 0)]
    weight_far = lax.ppermute(out_weight, "core", swap)

    in_tile = hilbert_order // image_width % TILE * TILE + hilbert_order % image_width % TILE
    places = jnp.stack([in_tile // TILE, in_tile % TILE]).reshape(8, HD)
    listed = jnp.pad(key_blocks, ((0, 7), (0, HD - SEL)))
    places = jnp.concatenate([places, listed]).astype(jnp.bfloat16)
    by_chunk = (16, -1, 2, TILES, TILE, HD)
    kv_rows = 2 * TILES * TILE * LEAD
    lead = exchange(pack(k_raster, v_raster, (0, LEAD), q_raster, places), BAND)
    numbers = lead[:, -16:].astype(jnp.int32)
    band_places = numbers[:, :8].reshape(16, 2, BLOCK)
    band_places = (band_places[:, 0] * TILE + band_places[:, 1]).reshape(TCOLS, 2, BLOCK)
    line_pos = lax.axis_index("zl")
    place = lax.dynamic_slice_in_dim(band_places, line_pos * TILES, TILES, axis=0)
    lead_ordered = order_kv(place, lead[:, :kv_rows].reshape(by_chunk))
    spread = swapped(lead_ordered, "x")
    spreads = [spread[:, c] for c in range(LEAD)]

    lists = lax.dynamic_slice_in_dim(numbers[:, 8, :SEL], line_pos * 4, 4, axis=0)
    lists = swapped(jnp.broadcast_to(lists[None], (4, 4, SEL)), "x")
    lists = lists[lax.axis_index("x") ^ jnp.arange(4)].reshape(16, SEL)

    side = lax.axis_index("yl")
    tile_places = lax.dynamic_index_in_dim(band_places, lax.axis_index(("zl", "yh")), 0, False)
    tile_places = jnp.where(side == 0, tile_places, tile_places[::-1])
    q_ordered = order_q(tile_places, lead[:, kv_rows:-16].reshape(16, -1, 2 * TILE, HD))
    q_other = lax.ppermute(q_ordered[1], "yl", swap)
    query = jnp.stack([q_ordered[0], q_other])
    flip = lax.axis_index("x").reshape(1)

    rest = exchange(after(pack(k_raster, v_raster, (LEAD, CHUNKS)), spread), BAND)
    ordered = order_kv(place, rest.reshape(by_chunk))
    pos = lax.axis_index(("yh", "yl"))
    ordered, _, _ = lax.optimization_barrier((ordered, lists, query))
    every = jnp.concatenate([lead_ordered, ordered], axis=1)
    own = [lax.dynamic_index_in_dim(every, pos ^ d, 2, False) for d in range(4)]
    later, own = lax.optimization_barrier(
        (swapped(ordered, "x"), swapped(own, ("yh", "yl")))
    )
    spreads += [later[:, c] for c in range(CHUNKS - LEAD)]
    held = [lax.all_gather(part, LINE, axis=0) for part in spreads]

    half = BLOCK // 2
    results = [jnp.zeros((half, out_weight.shape[1]), jnp.float32)]
    for c in range(CHUNKS):
        ready = after(lists, *((results[c - 1],) if c > 1 else (later,)))
        got = exchange(select(ready, flip, held[c]), PLANE)
        got = got.reshape(4, 2, 2, (SEL - 1) * PART, HD)
        attended = attend(pos.reshape(1), query, got, own, c)
        mine = lax.dynamic_slice_in_dim(attended, core * half, half, axis=0)
        theirs = lax.dynamic_slice_in_dim(attended, (1 - core) * half, half, axis=0)
        other = lax.ppermute(theirs, "core", swap)
        feats = slice(2 * c * HD, 2 * (c + 1) * HD)
        result = results[c] + jnp.dot(mine, out_weight[feats], preferred_element_type=jnp.float32)
        result += jnp.dot(other, weight_far[feats], preferred_element_type=jnp.float32)
        results.append(result)
    return results[-1].astype(jnp.bfloat16)


def solution(mesh):
    split = Mesh(mesh.devices.reshape(SIZES), SEQ + ("core",))
    placed = (
        P(SEQ, "core"),
        P(SEQ, "core"),
        P(SEQ, "core"),
        P(SEQ),
        P(SEQ, None),
        P("core", None),
    )
    return jax.shard_map(
        body, mesh=split, in_specs=placed, out_specs=P(SEQ + ("core",), None), check_vma=False
    )
```

```python
import functools
import itertools
import math

import jax
import jax.numpy as jnp
from jax import lax
from jax.experimental import pallas as pl
from jax.experimental.pallas import tpu as pltpu
from jax.sharding import Mesh, PartitionSpec as P

TILE = 32
TCOLS = 8
HD = 128
SEL = 8
BLOCK = 512
PART = 128
SEQ = ("x", "zh", "zl", "yh", "yl")
LINE = ("zh", "zl")
PLANE = ("x", "yh", "yl")
BAND = ("zl", "yh", "yl")
SIZES = (4, 2, 4, 2, 2, 2)
CHUNKS = 4
LEAD = 1
TILES = 2
VMEM_LIMIT = 48 * 1024 * 1024


def exchange(value, axes):
    return lax.all_to_all(value, axes, split_axis=0, concat_axis=0, tiled=True)


def after(value, *earlier):
    return lax.optimization_barrier((value,) + earlier)[0]


def swapped(pieces, axes):
    moved = [
        lax.ppermute(pieces[d], axes, [(i, i ^ d) for i in range(4)]) if d else pieces[0]
        for d in range(4)
    ]
    return jnp.stack(moved)


def picked(row, width):
    col = jnp.transpose(jnp.broadcast_to(row, (128, BLOCK)))
    lane = lax.broadcasted_iota(jnp.int32, (BLOCK, 128), 1)
    parts = [
        jnp.where(col == lane + 128 * k, 1.0, 0.0).astype(jnp.bfloat16) for k in range(width // 128)
    ]
    return jnp.concatenate(parts, axis=1)


def pack_kernel(k_ref, v_ref, *refs, chunks):
    out_ref = refs[-1]
    line_rows = TILE * TCOLS
    pair = TILES * TILE
    for dest in range(16):
        group, head, kv = dest // 4, dest // 2 % 2, dest % 2
        from_ref = v_ref if kv else k_ref
        at = 0
        for c, line in itertools.product(range(chunks[0], chunks[1]), range(2)):
            cols = pl.ds((2 * (c - chunks[0]) + head) * HD, HD)
            rows = pl.ds(line * line_rows + group * pair, pair)
            out_ref[dest, pl.ds(at, pair), :] = from_ref[rows, cols]
            at += pair
        if len(refs) == 3:
            q_ref, places_ref = refs[:2]
            for h, line in itertools.product(range(4), range(2)):
                rows = pl.ds(line * line_rows + (dest // 2) * TILE, TILE)
                out_ref[dest, pl.ds(at, TILE), :] = q_ref[rows, pl.ds((4 * kv + h) * HD, HD)]
                at += TILE
            out_ref[dest, pl.ds(at, 16), :] = places_ref[...]


def pack(keys, values, chunks, *more):
    width = 2 * HD * (chunks[1] - chunks[0])
    part = pl.BlockSpec((BLOCK, width), lambda g: (0, 0))
    rows = 2 * TILES * TILE * (chunks[1] - chunks[0])
    more_specs = [pl.BlockSpec(m.shape, lambda g: (0, 0)) for m in more]
    if more:
        rows += 8 * TILE + 16
    if chunks[0]:
        keys, values = keys[:, chunks[0] * 2 * HD :], values[:, chunks[0] * 2 * HD :]
    return pl.pallas_call(
        functools.partial(pack_kernel, chunks=chunks),
        grid=(1,),
        in_specs=[part, part] + more_specs,
        out_specs=pl.BlockSpec((16, rows, HD), lambda g: (0, 0, 0)),
        out_shape=jax.ShapeDtypeStruct((16, rows, HD), jnp.bfloat16),
        compiler_params=pltpu.CompilerParams(vmem_limit_bytes=VMEM_LIMIT),
        cost_estimate=pl.CostEstimate(
            flops=0, bytes_accessed=2 * 16 * rows * HD * 2, transcendentals=0
        ),
        name="pack",
    )(keys, values, *more)


def order_kv_kernel(place_ref, rows_ref, out_ref):
    tile = rows_ref[...].reshape(TILE * TILE, HD)
    for b in range(2):
        hot = picked(place_ref[0, b : b + 1, :], TILE * TILE)
        rows = jnp.dot(hot, tile, preferred_element_type=jnp.float32).astype(jnp.bfloat16)
        out_ref[:, 0, b] = rows.reshape(4, PART, HD)


def order_kv(place, rows):
    chunks = rows.shape[1]
    return pl.pallas_call(
        order_kv_kernel,
        grid=(chunks, TILES),
        in_specs=[
            pl.BlockSpec((1, 2, BLOCK), lambda c, t: (t, 0, 0)),
            pl.BlockSpec((16, 1, 2, 1, TILE, HD), lambda c, t: (0, c, 0, t, 0, 0)),
        ],
        out_specs=pl.BlockSpec((4, 1, 2, PART, HD), lambda c, t: (0, c, t, 0, 0)),
        out_shape=jax.ShapeDtypeStruct((4, chunks, 2 * TILES, PART, HD), jnp.bfloat16),
        compiler_params=pltpu.CompilerParams(vmem_limit_bytes=VMEM_LIMIT),
        cost_estimate=pl.CostEstimate(
            flops=chunks * TILES * 4 * BLOCK * TILE * TILE * HD,
            bytes_accessed=chunks * TILES * 2**19,
            transcendentals=0,
        ),
        name="order_kv",
    )(place, rows)


def order_q_kernel(place_ref, rows_ref, out_ref):
    tile = rows_ref[...].reshape(TILE * TILE, HD)
    for b in range(2):
        hot = picked(place_ref[b : b + 1, :], TILE * TILE)
        out_ref[b, 0] = jnp.dot(hot, tile, preferred_element_type=jnp.float32).astype(jnp.bfloat16)


def order_q(place, rows):
    heads = rows.shape[1]
    return pl.pallas_call(
        order_q_kernel,
        grid=(heads,),
        in_specs=[
            pl.BlockSpec((2, BLOCK), lambda t: (0, 0)),
            pl.BlockSpec((16, 1, 2 * TILE, HD), lambda t: (0, t, 0, 0)),
        ],
        out_specs=pl.BlockSpec((2, 1, BLOCK, HD), lambda t: (0, t, 0, 0)),
        out_shape=jax.ShapeDtypeStruct((2, heads, BLOCK, HD), jnp.bfloat16),
        compiler_params=pltpu.CompilerParams(vmem_limit_bytes=VMEM_LIMIT),
        cost_estimate=pl.CostEstimate(
            flops=heads * 4 * BLOCK * TILE * TILE * HD, bytes_accessed=2**21, transcendentals=0
        ),
        name="order_q",
    )(place, rows)


def select_kernel(blocks_ref, flip_ref, held_ref, out_ref, sem):
    def send(reader, carry):
        for slot in range(1, SEL):
            block = blocks_ref[reader, slot]
            col = lax.shift_right_logical(block, 5) ^ flip_ref[0]
            line = lax.shift_right_logical(block, 2) & 7
            pltpu.make_async_copy(
                held_ref.at[line, col, block & 3], out_ref.at[reader, slot - 1], sem
            ).start()
        return carry

    lax.fori_loop(0, 16, send, 0)
    pltpu.make_async_copy(out_ref, out_ref, sem).wait()


def select(blocks, flip, held):
    shape = (16, SEL - 1, PART, HD)
    return pl.pallas_call(
        select_kernel,
        grid_spec=pltpu.PrefetchScalarGridSpec(
            num_scalar_prefetch=2,
            grid=(1,),
            in_specs=[pl.BlockSpec(memory_space=pl.ANY)],
            out_specs=pl.BlockSpec(shape, lambda g, blocks, flip: (0, 0, 0, 0)),
            scratch_shapes=[pltpu.SemaphoreType.DMA],
        ),
        out_shape=jax.ShapeDtypeStruct(shape, jnp.bfloat16),
        compiler_params=pltpu.CompilerParams(vmem_limit_bytes=VMEM_LIMIT),
        cost_estimate=pl.CostEstimate(flops=0, bytes_accessed=2**23, transcendentals=0),
        name="select",
    )(blocks, flip, held)


def attend_kernel(pos_ref, q_ref, k_ref, v_ref, own_k_ref, own_v_ref, out_ref, *, scale):
    query = q_ref[0, 0]
    top = jnp.full((BLOCK, 1), -jnp.inf, jnp.float32)
    total = jnp.zeros((BLOCK, 1), jnp.float32)
    mixed = jnp.zeros((BLOCK, HD), jnp.float32)
    for c in range(4):
        keys = jnp.concatenate([k_ref[c, 0, 0], own_k_ref[0, c, 0]])
        values = jnp.concatenate([v_ref[c, 0, 0], own_v_ref[0, c, 0]])
        scores = lax.dot_general(
            query, keys, (((1,), (1,)), ((), ())), preferred_element_type=jnp.float32
        )
        peak = jnp.maximum(top, jnp.max(scores, axis=1, keepdims=True))
        weights = jnp.exp2(scores * scale - peak * scale)
        fade = jnp.exp2((top - peak) * scale)
        total = total * fade + jnp.sum(weights, axis=1, keepdims=True)
        mixed = mixed * fade + jnp.dot(
            weights.astype(jnp.bfloat16), values, preferred_element_type=jnp.float32
        )
        top = peak
    out_ref[...] = (mixed / total).astype(jnp.bfloat16)


def attend(pos, query, fetched, own, chunk):
    rows = (SEL - 1) * PART
    spec = (4, 1, 1, rows, HD)
    own_spec = (1, 4, 1, PART, HD)
    heads = 2
    per_side = query.shape[1]
    first = heads * chunk
    return pl.pallas_call(
        functools.partial(attend_kernel, scale=math.log2(math.e) / math.sqrt(HD)),
        grid_spec=pltpu.PrefetchScalarGridSpec(
            num_scalar_prefetch=1,
            grid=(heads,),
            in_specs=[
                pl.BlockSpec(
                    (1, 1, BLOCK, HD),
                    lambda g, pos: (first // per_side ^ (pos[0] & 1), first % per_side + g, 0, 0),
                ),
                pl.BlockSpec(spec, lambda g, pos: (0, g, 0, 0, 0)),
                pl.BlockSpec(spec, lambda g, pos: (0, g, 1, 0, 0)),
                pl.BlockSpec(own_spec, lambda g, pos: ((2 * g) ^ pos[0], 0, chunk, 0, 0)),
                pl.BlockSpec(own_spec, lambda g, pos: ((2 * g + 1) ^ pos[0], 0, chunk, 0, 0)),
            ],
            out_specs=pl.BlockSpec((BLOCK, HD), lambda g, pos: (0, g)),
        ),
        out_shape=jax.ShapeDtypeStruct((BLOCK, heads * HD), jnp.bfloat16),
        compiler_params=pltpu.CompilerParams(vmem_limit_bytes=VMEM_LIMIT),
        cost_estimate=pl.CostEstimate(
            flops=heads * 4 * BLOCK * BLOCK * SEL * HD * 4,
            bytes_accessed=heads * 2**21,
            transcendentals=heads * BLOCK * BLOCK * SEL,
        ),
        name="attend",
    )(pos, query, fetched, fetched, own, own)


def body(q_raster, k_raster, v_raster, hilbert_order, key_blocks, out_weight):
    width = q_raster.shape[1]
    image_width = TILE * TCOLS
    core = lax.axis_index("core")
    swap = [(0, 1), (1, 0)]
    weight_far = lax.ppermute(out_weight, "core", swap)

    in_tile = hilbert_order // image_width % TILE * TILE + hilbert_order % image_width % TILE
    places = jnp.stack([in_tile // TILE, in_tile % TILE]).reshape(8, HD)
    listed = jnp.pad(key_blocks, ((0, 7), (0, HD - SEL)))
    places = jnp.concatenate([places, listed]).astype(jnp.bfloat16)
    by_chunk = (16, -1, 2, TILES, TILE, HD)
    kv_rows = 2 * TILES * TILE * LEAD
    lead = exchange(pack(k_raster, v_raster, (0, LEAD), q_raster, places), BAND)
    numbers = lead[:, -16:].astype(jnp.int32)
    band_places = numbers[:, :8].reshape(16, 2, BLOCK)
    band_places = (band_places[:, 0] * TILE + band_places[:, 1]).reshape(TCOLS, 2, BLOCK)
    line_pos = lax.axis_index("zl")
    place = lax.dynamic_slice_in_dim(band_places, line_pos * TILES, TILES, axis=0)
    lead_ordered = order_kv(place, lead[:, :kv_rows].reshape(by_chunk))
    spread = swapped(lead_ordered, "x")
    spreads = [spread[:, c] for c in range(LEAD)]

    lists = lax.dynamic_slice_in_dim(numbers[:, 8, :SEL], line_pos * 4, 4, axis=0)
    lists = swapped(jnp.broadcast_to(lists[None], (4, 4, SEL)), "x")
    lists = lists[lax.axis_index("x") ^ jnp.arange(4)].reshape(16, SEL)

    side = lax.axis_index("yl")
    tile_places = lax.dynamic_index_in_dim(band_places, lax.axis_index(("zl", "yh")), 0, False)
    tile_places = jnp.where(side == 0, tile_places, tile_places[::-1])
    q_ordered = order_q(tile_places, lead[:, kv_rows:-16].reshape(16, -1, 2 * TILE, HD))
    q_other = lax.ppermute(q_ordered[1], "yl", swap)
    query = jnp.stack([q_ordered[0], q_other])
    flip = lax.axis_index("x").reshape(1)

    rest = exchange(after(pack(k_raster, v_raster, (LEAD, CHUNKS)), spread), BAND)
    ordered = order_kv(place, rest.reshape(by_chunk))
    pos = lax.axis_index(("yh", "yl"))
    ordered, _, _ = lax.optimization_barrier((ordered, lists, query))
    every = jnp.concatenate([lead_ordered, ordered], axis=1)
    own = [lax.dynamic_index_in_dim(every, pos ^ d, 2, False) for d in range(4)]
    later = swapped(ordered, "x")
    own = swapped(own, ("yh", "yl"))
    spreads += [later[:, c] for c in range(CHUNKS - LEAD)]
    held = [lax.all_gather(part, LINE, axis=0) for part in spreads]

    half = BLOCK // 2
    results = [jnp.zeros((half, out_weight.shape[1]), jnp.float32)]
    for c in range(CHUNKS):
        ready = after(lists, *((results[c - 1],) if c > 1 else (later, own)))
        got = exchange(select(ready, flip, held[c]), PLANE)
        got = got.reshape(4, 2, 2, (SEL - 1) * PART, HD)
        attended = attend(pos.reshape(1), query, got, own, c)
        mine = lax.dynamic_slice_in_dim(attended, core * half, half, axis=0)
        theirs = lax.dynamic_slice_in_dim(attended, (1 - core) * half, half, axis=0)
        other = lax.ppermute(theirs, "core", swap)
        feats = slice(2 * c * HD, 2 * (c + 1) * HD)
        result = results[c] + jnp.dot(mine, out_weight[feats], preferred_element_type=jnp.float32)
        result += jnp.dot(other, weight_far[feats], preferred_element_type=jnp.float32)
        results.append(result)
    return results[-1].astype(jnp.bfloat16)


def solution(mesh):
    split = Mesh(mesh.devices.reshape(SIZES), SEQ + ("core",))
    placed = (
        P(SEQ, "core"),
        P(SEQ, "core"),
        P(SEQ, "core"),
        P(SEQ),
        P(SEQ, None),
        P("core", None),
    )
    return jax.shard_map(
        body, mesh=split, in_specs=placed, out_specs=P(SEQ + ("core",), None), check_vma=False
    )
```
